32 devices in a mesh: leaf: 8 (over z, core), gen: 4 (over y, x).
Axes of the slice: x: 2, y: 2, z: 4, core: 2. Of those that a mesh axis runs over, the one named last changes fastest.
Arguments:
- points: float32 [16, 8, 2, 512], P(None, 'leaf'), may hold values from 0 to 1
- generators: bfloat16 [16, 8, 2, 512, 128], P(None, 'leaf', None, 'gen'), may hold values from -6 to 6
- leaf_ranks: int32 [16, 8], P(None, 'leaf'), may hold values from 112 to 128
- translations: bfloat16 [16, 8, 128, 256], P(None, 'leaf'), may hold values from -0.5 to 0.5
- parent_ranks: int32 [8, 8], P(None, 'leaf'), may hold values from 128 to 160
Outputs:
- leaf_basis: float32 [16, 8, 2, 512, 128], P(None, 'leaf', None, 'gen')
- leaf_block: float32 [16, 8, 128, 128], P(None, 'leaf', 'gen')
- parent_basis: float32 [8, 8, 256, 256], P(None, 'leaf', 'gen')
- parent_block: float32 [8, 8, 256, 256], P(None, 'leaf', 'gen')
The draws below stay inside these ranges and needn't reach their ends.
Inputs may be any that keep to these rules, and one draw needn't show every extreme that they name: `leaf_ranks`: a leaf's rank; generator columns from the rank on are ignored. `parent_ranks`: a parent's rank; translation columns from the rank on are ignored.
All inputs are finite; a program needn't handle non-finite values.
Results may differ from the reference program's by a relative error of at most 0.0003.
Values may be sent and summed in bfloat16 or wider, within the bound.
A program may use at most 128 MiB of HBM per device.

```python
import jax
import jax.numpy as jnp
from jax import lax

PTS = 512
KL = 128
KP = 256
LEAF_DEV = 16
GROUPS = 8
HALF = 8


def place_ends(array, key, least, high):
    shape = array.shape
    place = [jax.random.randint(jax.random.fold_in(key, axis), (), 0, shape[axis]) for axis in range(len(shape))]
    array = array.at[tuple(place)].set(least)
    longest = shape.index(max(shape))
    place[longest] = (place[longest] + 1) % shape[longest]
    return array.at[tuple(place)].set(high)


def shard_levels(rng, dims, cuts, smallest, top_value):
    level, own = 1.0, jax.random.fold_in(rng, 6)
    for dim, parts in cuts:
        steps = jnp.exp(jax.random.uniform(jax.random.fold_in(own, dim), (parts,), jnp.float32, smallest / len(cuts), top_value / len(cuts)))
        level = level * jnp.repeat(steps, dims[dim] // parts).reshape([-1 if axis == dim else 1 for axis in range(len(dims))])
    return level


def scatter_about(key, dims, spread, reach, pieces=(), held_as=jnp.bfloat16):
    loudness = shard_levels(key, dims, pieces, -0.22, 0.18) if pieces else 1.0
    array = jax.random.normal(key, dims, jnp.float32) * spread * loudness
    return jnp.minimum(jnp.maximum(array, -reach), reach).astype(held_as)


def setup_inputs(seed: int = 0) -> dict:
    key_of = jax.random.split(jax.random.key(seed), 6)
    points = jnp.clip(1.0 * jax.random.uniform(key_of[0], (LEAF_DEV, GROUPS, 2, PTS), jnp.float32) ** shard_levels(key_of[0], (LEAF_DEV, GROUPS, 2, PTS), ((1, 8),), -0.2, 0.2), 0.0, 1.0)
    generators = scatter_about(key_of[1], (LEAF_DEV, GROUPS, 2, PTS, KL), 1.0, 6.0, ((1, 8), (3, 4)))
    leaf_ranks = place_ends(jax.random.randint(key_of[2], (LEAF_DEV, GROUPS), KL * 7 // 8, KL + 1), jax.random.fold_in(key_of[2], 1), KL * 7 // 8, KL).astype(jnp.int32)
    translations = scatter_about(key_of[3], (LEAF_DEV, GROUPS, KL, KP), KL ** -0.5, 0.5, ((1, 8),))
    parent_ranks = place_ends(jax.random.randint(key_of[4], (HALF, GROUPS), KP // 2, KP * 5 // 8 + 1), jax.random.fold_in(key_of[4], 1), KP // 2, (KP * 5 // 8 + 1) - 1).astype(jnp.int32)
    return {"points": points, "generators": generators, "leaf_ranks": leaf_ranks, "translations": translations, "parent_ranks": parent_ranks}


HIGHEST = lax.Precision.HIGHEST
RANGE_SCALE = 4.0
SIGMA_ONE = 1.0
SIGMA_TWO = 0.8
CROSS_CORR = 0.5
NUGGET = 0.1

def matern(first, second):
    across = first[..., 0, :, None] - second[..., 0, None, :]
    upward = first[..., 1, :, None] - second[..., 1, None, :]
    scaled = RANGE_SCALE * jnp.sqrt(across * across + upward * upward)
    decays = jnp.exp(-scaled)
    marginal_one = SIGMA_ONE * SIGMA_ONE * decays
    middle = CROSS_CORR * SIGMA_ONE * SIGMA_TWO * (1.0 + scaled) * decays
    smooth = SIGMA_TWO * SIGMA_TWO * (1.0 + scaled + scaled * scaled / 3.0) * decays
    top_row = jnp.stack([marginal_one, middle], -2)
    bottom_row = jnp.stack([middle, smooth], -2)
    return jnp.stack([top_row, bottom_row], -4)

def reference(points, generators, leaf_ranks, translations, parent_ranks):
    total = LEAF_DEV * GROUPS
    flat_points = points.reshape(total, 2, PTS)
    flat_gen = generators.reshape(total, 2, PTS, KL)
    flat_ranks = leaf_ranks.reshape(total)
    flat_maps = translations.reshape(total, KL, KP)
    identity = jnp.eye(KL, dtype=jnp.float32)

    def leaf_work(member):
        coords, shard, leaf_rank, mapping = member
        column_keep = (lax.iota(jnp.int32, KL) < leaf_rank).astype(jnp.float32)
        flat_rows = (shard.astype(jnp.float32) * column_keep).reshape(2 * PTS, KL)
        gram_sum = jnp.dot(flat_rows.T, flat_rows, precision=HIGHEST) + jnp.diag(1.0 - column_keep)
        factor_low = jnp.linalg.cholesky(gram_sum)
        inverse = jax.scipy.linalg.solve_triangular(factor_low, identity, lower=True)
        bases = jnp.dot(flat_rows, inverse.T, precision=HIGHEST).reshape(2, PTS, KL)
        images = jnp.einsum('vnwp,wpk->vnk', matern(coords, coords), bases, precision=HIGHEST) + NUGGET * bases
        block = jnp.einsum('vnk,vnj->kj', bases, images, precision=HIGHEST)
        factor = jnp.dot(factor_low.T, mapping.astype(jnp.float32) * column_keep[:, None], precision=HIGHEST)
        return (bases, block, factor)
    all_bases, all_blocks, all_factors = lax.map(leaf_work, (flat_points, flat_gen, flat_ranks, flat_maps))
    parent_identity = jnp.eye(KP, dtype=jnp.float32)

    def parent_work(member):
        index, parent_rank = member
        slot_index = index % GROUPS % 2 * HALF + index // GROUPS
        even_leaf = (slot_index * GROUPS + index % GROUPS // 2 * 2).astype(jnp.int32)
        odd_leaf = even_leaf + 1
        reaches = jnp.einsum('vnwp,wpk->vnk', matern(flat_points[even_leaf], flat_points[odd_leaf]), all_bases[odd_leaf], precision=HIGHEST)
        coupled = jnp.einsum('vnk,vnj->kj', all_bases[even_leaf], reaches, precision=HIGHEST)
        parent_keep = (lax.iota(jnp.int32, KP) < parent_rank).astype(jnp.float32)
        stacked = jnp.concatenate([all_factors[even_leaf], all_factors[odd_leaf]], 0) * parent_keep[None, :]
        parent_gram = jnp.dot(stacked.T, stacked, precision=HIGHEST) + jnp.diag(1.0 - parent_keep)
        parent_low = jnp.linalg.cholesky(parent_gram)
        parent_inverse = jax.scipy.linalg.solve_triangular(parent_low, parent_identity, lower=True)
        parent_bases = jnp.dot(stacked, parent_inverse.T, precision=HIGHEST)
        top_row = jnp.concatenate([all_blocks[even_leaf], coupled], 1)
        bottom_row = jnp.concatenate([coupled.T, all_blocks[odd_leaf]], 1)
        parent_matrix = jnp.concatenate([top_row, bottom_row], 0)
        projected = jnp.dot(parent_bases.T, jnp.dot(parent_matrix, parent_bases, precision=HIGHEST), precision=HIGHEST)
        return (parent_bases, projected)
    indices = lax.iota(jnp.int32, HALF * GROUPS)
    parent_bases, parent_blocks = lax.map(parent_work, (indices, parent_ranks.reshape(HALF * GROUPS)))
    return (all_bases.reshape(LEAF_DEV, GROUPS, 2, PTS, KL), all_blocks.reshape(LEAF_DEV, GROUPS, KL, KL), parent_bases.reshape(HALF, GROUPS, 2 * KL, KP), parent_blocks.reshape(HALF, GROUPS, KP, KP))
```

```python
import functools

import jax
import jax.numpy as jnp
from jax import lax
from jax.experimental import pallas as pl
from jax.experimental.pallas import tpu as pltpu
from jax.sharding import PartitionSpec as P

HIGHEST = lax.Precision.HIGHEST
RANGE_SCALE = 4.0
SIGMA_ONE = 1.0
SIGMA_TWO = 0.8
CROSS_CORR = 0.5
NUGGET = 0.1
BLOCK = 32


def swapped(array):
    return lax.ppermute(array, "leaf", [(i, i ^ 1) for i in range(lax.axis_size("leaf"))])


def eliminate(steps, gram_ref, upper_ref, inverse_ref, work_ref):
    count, rows, width = gram_ref.shape
    lanes = lax.broadcasted_iota(jnp.int32, (1, width), 1)
    work_ref[...] = gram_ref[:, :steps, :]
    if steps < rows:
        upper_ref[:, steps:, :] = jnp.zeros((count, rows - steps, width), jnp.float32)
        inverse_ref[:, steps:, :] = jnp.zeros((count, rows - steps, width), jnp.float32)

    for start in range(0, steps, BLOCK):

        def step(k, carry, start=start):
            here = lanes == k
            for b in range(count):
                row = work_ref[b, pl.ds(k, 1), :]
                below = work_ref[b, start:, :]
                pivot = jnp.sum(jnp.where(here, row, 0.0), axis=1, keepdims=True)
                column = jnp.sum(jnp.where(here, below, 0.0), axis=1, keepdims=True)
                root = lax.rsqrt(pivot)
                root = root * (1.5 - 0.5 * pivot * root * root)
                upper_ref[b, pl.ds(k, 1), :] = jnp.where(lanes >= k, row, 0.0) * root
                one = jnp.where(here, 1.0, 0.0)
                inverse_ref[b, pl.ds(k, 1), :] = jnp.where(lanes < k, row, one) * root
                scaled = column * (root * root)
                work_ref[b, start:, :] = jnp.where(here, -scaled, below - scaled * row)
            return carry

        lax.fori_loop(start, start + BLOCK, step, 0)


def factor(gram, steps):
    shape = jax.ShapeDtypeStruct(gram.shape, jnp.float32)
    count, _, width = gram.shape
    return pl.pallas_call(
        functools.partial(eliminate, steps),
        out_shape=(shape, shape),
        scratch_shapes=[pltpu.VMEM((count, steps, width), jnp.float32)],
    )(gram)


def split(value):
    high = value.astype(jnp.bfloat16)
    return high, (value - high.astype(jnp.float32)).astype(jnp.bfloat16)


def times(value, exact):
    high, low = split(value)
    return jnp.dot(high, exact, preferred_element_type=jnp.float32) + jnp.dot(
        low, exact, preferred_element_type=jnp.float32
    )


def gather_covariance(near_ref, far_ref, near_rows_ref, far_rows_ref, out_ref):
    @pl.when(pl.program_id(1) == 0)
    def _():
        out_ref[...] = jnp.zeros_like(out_ref)

    near = near_ref[0]
    far = far_ref[0]
    across = near[:, 0:1] - far[0:1, :]
    upward = near[:, 1:2] - far[1:2, :]
    scaled = RANGE_SCALE * jnp.sqrt(across * across + upward * upward)
    decays = jnp.exp(-scaled)
    one = SIGMA_ONE * SIGMA_ONE * decays
    middle = (CROSS_CORR * SIGMA_ONE * SIGMA_TWO) * (1.0 + scaled) * decays
    smooth = (SIGMA_TWO * SIGMA_TWO) * (1.0 + scaled + scaled * scaled * (1.0 / 3.0)) * decays
    first, second = far_rows_ref[0, 0], far_rows_ref[0, 1]
    top = times(one, first) + times(middle, second)
    bottom = times(middle, first) + times(smooth, second)
    total = out_ref[0]
    for variable, image in ((0, top), (1, bottom)):
        for part in split(image):
            total = total + lax.dot_general(
                near_rows_ref[0, variable], part, (((0,), (0,)), ((), ())),
                preferred_element_type=jnp.float32,
            )
    out_ref[0] = total


def covariance(near_coords, far_coords, near_rows, far_rows):
    count, _, points, width = near_rows.shape
    tile = 128
    return pl.pallas_call(
        gather_covariance,
        grid=(count, points // tile),
        in_specs=[
            pl.BlockSpec((1, tile, 2), lambda i, j: (i, j, 0)),
            pl.BlockSpec((1, 2, points), lambda i, j: (i, 0, 0)),
            pl.BlockSpec((1, 2, tile, width), lambda i, j: (i, 0, j, 0)),
            pl.BlockSpec((1, 2, points, width), lambda i, j: (i, 0, 0, 0)),
        ],
        out_specs=pl.BlockSpec((1, width, width), lambda i, j: (i, 0, 0)),
        out_shape=jax.ShapeDtypeStruct((count, width, width), jnp.float32),
    )(jnp.swapaxes(near_coords, 1, 2), far_coords, near_rows, far_rows)


def sandwich(left, inner, right):
    mixed = jnp.einsum("lab,lcb->lac", inner, right, precision=HIGHEST)
    return jnp.einsum("lka,lac->lkc", left, mixed, precision=HIGHEST)


def per_device(points, generators, leaf_ranks, translations, parent_ranks):
    leaf_count, _, _, row_share, rank_width = generators.shape
    point_count = points.shape[-1]
    half = leaf_count // 2
    parent_width = translations.shape[-1]
    parent_most = parent_width * 5 // 8
    gens = lax.axis_size("gen")
    spot = lax.axis_index("gen")
    parity = lax.axis_index("leaf") % 2
    is_even = parity == 0
    sides = 2 if leaf_count // gens % 2 == 0 else 1
    each = leaf_count // (gens * sides)
    owned = sides * each

    def mine(values):
        values = values.reshape(sides, gens, each, *values.shape[1:])
        values = lax.dynamic_index_in_dim(values, spot, 1, keepdims=False)
        return values.reshape(owned, *values.shape[2:])

    def side(values, index):
        if sides == 1:
            return values
        return lax.dynamic_slice_in_dim(values, index * each, each, 0)

    local = generators[:, 0]
    spread = local.reshape(sides, gens, each, 2, row_share, rank_width)
    rows = lax.all_to_all(spread, "gen", split_axis=1, concat_axis=4, tiled=True)
    rows = rows.reshape(owned, 2, point_count, rank_width)
    coords = mine(points[:, 0])
    keep = (lax.iota(jnp.int32, rank_width)[None, :] < mine(leaf_ranks[:, 0])[:, None]).astype(
        jnp.float32
    )
    far_rows = swapped(side(rows, 1 - parity))
    far_coords = swapped(side(coords, 1 - parity))
    full = jnp.einsum("lvnk,lvnj->lkj", rows, rows, preferred_element_type=jnp.float32)
    eye = jnp.eye(rank_width, dtype=jnp.float32)
    gram = full * keep[:, :, None] * keep[:, None, :] + eye * (1.0 - keep)[:, None, :]
    upper, inverse = factor(gram, rank_width)
    upper = upper * keep[:, :, None]
    inverse = inverse * keep[:, :, None]
    every = lax.all_gather(inverse.reshape(sides, each, rank_width, rank_width), "gen", axis=1)
    every = every.reshape(leaf_count, rank_width, rank_width)

    factors = jnp.einsum(
        "lkj,ljp->lkp", upper, mine(translations[:, 0]).astype(jnp.float32), precision=HIGHEST
    )
    sums = covariance(
        jnp.concatenate([coords, side(coords, parity)], 0),
        jnp.concatenate([coords, far_coords], 0),
        jnp.concatenate([rows, side(rows, parity)], 0),
        jnp.concatenate([rows, far_rows], 0),
    )
    blocks = sandwich(inverse, sums[:owned] + NUGGET * full, inverse)
    bases = jnp.einsum(
        "lvnk,ljk->lvnj", local, every, precision=HIGHEST, preferred_element_type=jnp.float32
    )

    given = jnp.concatenate([factors, blocks, inverse], 2)
    far = swapped(side(given, 1 - parity))
    own_factor, own_block = side(factors, parity), side(blocks, parity)
    far_factor = far[:, :, :parent_width]
    far_block = far[:, :, parent_width : parent_width + rank_width]
    far_inverse = far[:, :, parent_width + rank_width :]
    coupled = sandwich(side(inverse, parity), sums[owned:], far_inverse)
    coupled = jnp.where(is_even, coupled, jnp.swapaxes(coupled, 1, 2))
    even_block = jnp.where(is_even, own_block, far_block)
    odd_block = jnp.where(is_even, far_block, own_block)
    even_factor = jnp.where(is_even, own_factor, far_factor)
    odd_factor = jnp.where(is_even, far_factor, own_factor)
    ranks = parent_ranks[:, 0]
    if sides == 1:
        other = swapped(ranks)
        ranks = jnp.where(
            is_even, jnp.concatenate([ranks, other]), jnp.concatenate([other, ranks])
        )
    ranks = lax.dynamic_slice_in_dim(ranks, spot * each, each, 0)
    parent_keep = (lax.iota(jnp.int32, parent_width)[None, :] < ranks[:, None]).astype(jnp.float32)
    stacked = jnp.concatenate([even_factor, odd_factor], 1) * parent_keep[:, None, :]
    parent_gram = jnp.einsum("lak,laj->lkj", stacked, stacked, precision=HIGHEST)
    parent_gram = parent_gram + jnp.eye(parent_width, dtype=jnp.float32) * (1.0 - parent_keep)[:, None, :]
    _, parent_inverse = factor(parent_gram, parent_most)
    parent_bases = jnp.einsum("lak,ljk->laj", stacked, parent_inverse, precision=HIGHEST)
    top_row = jnp.concatenate([even_block, coupled], 2)
    bottom_row = jnp.concatenate([jnp.swapaxes(coupled, 1, 2), odd_block], 2)
    parent_matrix = jnp.concatenate([top_row, bottom_row], 1)
    mixed = jnp.einsum("lab,lbj->laj", parent_matrix, parent_bases, precision=HIGHEST)
    parent_blocks = jnp.einsum("lak,laj->lkj", parent_bases, mixed, precision=HIGHEST)

    leaf_share = rank_width // gens
    basis_share = 2 * rank_width // gens
    parent_share = parent_width // gens
    lanes = 128
    tiles = parent_width // lanes

    def packed(values, share):
        values = values.reshape(each, gens, share, tiles, lanes)
        return values.transpose(1, 0, 3, 2, 4).reshape(gens, each * tiles * share, lanes)

    def unpacked(values, share):
        values = values.reshape(gens * each, tiles, share, lanes)
        if sides == 1:
            values = lax.dynamic_slice_in_dim(values, parity * half, half, 0)
        return values.transpose(0, 2, 1, 3).reshape(half, share, parent_width)

    leaf_pack = blocks.reshape(owned, gens, leaf_share, rank_width).transpose(1, 0, 2, 3)
    leaf_pack = leaf_pack.reshape(gens, owned * leaf_share, rank_width)
    pack = jnp.concatenate(
        [leaf_pack, packed(parent_bases, basis_share), packed(parent_blocks, parent_share)], 1
    )
    pack = lax.all_to_all(pack, "gen", split_axis=0, concat_axis=0, tiled=True)
    first = owned * leaf_share
    second = first + each * tiles * basis_share
    leaf_out = pack[:, :first].reshape(gens, sides, each, leaf_share, rank_width)
    leaf_out = leaf_out.transpose(1, 0, 2, 3, 4).reshape(leaf_count, leaf_share, rank_width)
    basis_out = unpacked(pack[:, first:second], basis_share)
    block_out = unpacked(pack[:, second:], parent_share)
    return (bases[:, None], leaf_out[:, None], basis_out[:, None], block_out[:, None])


def solution(mesh):
    return jax.shard_map(
        per_device,
        mesh=mesh,
        in_specs=(
            P(None, "leaf", None, None),
            P(None, "leaf", None, "gen", None),
            P(None, "leaf"),
            P(None, "leaf", None, None),
            P(None, "leaf"),
        ),
        out_specs=(
            P(None, "leaf", None, "gen", None),
            P(None, "leaf", "gen", None),
            P(None, "leaf", "gen", None),
            P(None, "leaf", "gen", None),
        ),
        check_vma=False,
    )
```

```python
import functools

import jax
import jax.numpy as jnp
from jax import lax
from jax.experimental import pallas as pl
from jax.experimental.pallas import tpu as pltpu
from jax.sharding import PartitionSpec as P

HIGHEST = lax.Precision.HIGHEST
RANGE_SCALE = 4.0
SIGMA_ONE = 1.0
SIGMA_TWO = 0.8
CROSS_CORR = 0.5
NUGGET = 0.1
BLOCK = 32
GROUP = 4
LANES = 128
TINY = 1e-30


def swapped(array):
    return lax.ppermute(array, "leaf", [(i, i ^ 1) for i in range(lax.axis_size("leaf"))])


def eliminate(steps, gram_ref, upper_ref, inverse_ref, work_ref):
    count, rows, width = gram_ref.shape
    lanes = lax.broadcasted_iota(jnp.int32, (1, 1, width), 2)
    work_ref[...] = gram_ref[:, :steps, :]
    if steps < rows:
        upper_ref[:, steps:, :] = jnp.zeros((count, rows - steps, width), jnp.float32)
        inverse_ref[:, steps:, :] = jnp.zeros((count, rows - steps, width), jnp.float32)

    for start in range(0, steps, BLOCK):
        tile = start // LANES * LANES

        def step(turn, carry, start=start, tile=tile):
            first = start + turn * GROUP
            here = [lanes == first + i for i in range(GROUP)]
            spot = [mark[:, :, tile : tile + LANES] for mark in here]
            below = work_ref[:, start:, :]
            rows = [work_ref[:, pl.ds(first + i, 1), :] for i in range(GROUP)]

            def pick(values, i):
                values = values[:, :, tile : tile + LANES]
                return jnp.sum(jnp.where(spot[i], values, 0.0), axis=2, keepdims=True)

            columns = [pick(below, i) for i in range(GROUP)]
            corner = [[pick(rows[i], j) if j >= i else None for j in range(GROUP)] for i in range(GROUP)]
            for i in range(GROUP):
                pivot, row = corner[i][i], rows[i]
                root = lax.rsqrt(pivot)
                root = root * (1.5 - 0.5 * pivot * root * root)
                recip = root * root
                upper_ref[:, pl.ds(first + i, 1), :] = jnp.where(lanes >= first + i, row, 0.0) * root
                one = jnp.where(here[i], 1.0, 0.0)
                inverse_ref[:, pl.ds(first + i, 1), :] = jnp.where(lanes < first + i, row, one) * root
                scaled = columns[i] * recip
                below = jnp.where(here[i], -scaled, below - scaled * row)
                for j in range(i + 1, GROUP):
                    ratio = corner[i][j] * recip
                    rows[j] = jnp.where(here[i], -ratio, rows[j] - ratio * row)
                    columns[j] = columns[j] - scaled * corner[i][j]
                    for m in range(j, GROUP):
                        corner[j][m] = corner[j][m] - ratio * corner[i][m]
            work_ref[:, start:, :] = below
            return carry

        lax.fori_loop(0, BLOCK // GROUP, step, 0)


def factor(gram, steps):
    shape = jax.ShapeDtypeStruct(gram.shape, jnp.float32)
    count, _, width = gram.shape
    return pl.pallas_call(
        functools.partial(eliminate, steps),
        out_shape=(shape, shape),
        scratch_shapes=[pltpu.VMEM((count, steps, width), jnp.float32)],
    )(gram)


def split(value):
    high = value.astype(jnp.bfloat16)
    return high, (value - high.astype(jnp.float32)).astype(jnp.bfloat16)


def times(value, exact):
    high, low = split(value)
    return jnp.dot(high, exact, preferred_element_type=jnp.float32) + jnp.dot(
        low, exact, preferred_element_type=jnp.float32
    )


def gather_covariance(near_ref, far_ref, near_rows_ref, far_rows_ref, out_ref):
    @pl.when(pl.program_id(1) == 0)
    def _():
        out_ref[...] = jnp.zeros_like(out_ref)

    near = near_ref[0]
    far = far_ref[0]
    across = near[:, 0:1] - far[0:1, :]
    upward = near[:, 1:2] - far[1:2, :]
    square = across * across + upward * upward
    scaled = RANGE_SCALE * square * lax.rsqrt(jnp.maximum(square, TINY))
    decays = jnp.exp(-scaled)
    one = SIGMA_ONE * SIGMA_ONE * decays
    middle = (CROSS_CORR * SIGMA_ONE * SIGMA_TWO) * (1.0 + scaled) * decays
    smooth = (SIGMA_TWO * SIGMA_TWO) * (1.0 + scaled + scaled * scaled * (1.0 / 3.0)) * decays
    first, second = far_rows_ref[0, 0], far_rows_ref[0, 1]
    top = times(one, first) + times(middle, second)
    bottom = times(middle, first) + times(smooth, second)
    total = out_ref[0]
    for variable, image in ((0, top), (1, bottom)):
        for part in split(image):
            total = total + lax.dot_general(
                near_rows_ref[0, variable], part, (((0,), (0,)), ((), ())),
                preferred_element_type=jnp.float32,
            )
    out_ref[0] = total


def covariance(near_coords, far_coords, near_rows, far_rows):
    count, _, points, width = near_rows.shape
    tile = 128
    return pl.pallas_call(
        gather_covariance,
        grid=(count, points // tile),
        in_specs=[
            pl.BlockSpec((1, tile, 2), lambda i, j: (i, j, 0)),
            pl.BlockSpec((1, 2, points), lambda i, j: (i, 0, 0)),
            pl.BlockSpec((1, 2, tile, width), lambda i, j: (i, 0, j, 0)),
            pl.BlockSpec((1, 2, points, width), lambda i, j: (i, 0, 0, 0)),
        ],
        out_specs=pl.BlockSpec((1, width, width), lambda i, j: (i, 0, 0)),
        out_shape=jax.ShapeDtypeStruct((count, width, width), jnp.float32),
    )(jnp.swapaxes(near_coords, 1, 2), far_coords, near_rows, far_rows)


def sandwich(left, inner, right):
    mixed = jnp.einsum("lab,lcb->lac", inner, right, precision=HIGHEST)
    return jnp.einsum("lka,lac->lkc", left, mixed, precision=HIGHEST)


def per_device(points, generators, leaf_ranks, translations, parent_ranks):
    leaf_count, _, _, row_share, rank_width = generators.shape
    point_count = points.shape[-1]
    half = leaf_count // 2
    parent_width = translations.shape[-1]
    parent_most = parent_width * 5 // 8
    gens = lax.axis_size("gen")
    spot = lax.axis_index("gen")
    parity = lax.axis_index("leaf") % 2
    is_even = parity == 0
    sides = 2 if leaf_count // gens % 2 == 0 else 1
    each = leaf_count // (gens * sides)
    owned = sides * each

    def mine(values):
        values = values.reshape(sides, gens, each, *values.shape[1:])
        values = lax.dynamic_index_in_dim(values, spot, 1, keepdims=False)
        return values.reshape(owned, *values.shape[2:])

    def side(values, index):
        if sides == 1:
            return values
        return lax.dynamic_slice_in_dim(values, index * each, each, 0)

    local = generators[:, 0]
    spread = local.reshape(sides, gens, each, 2, row_share, rank_width)
    rows = lax.all_to_all(spread, "gen", split_axis=1, concat_axis=4, tiled=True)
    rows = rows.reshape(owned, 2, point_count, rank_width)
    coords = mine(points[:, 0])
    keep = (lax.iota(jnp.int32, rank_width)[None, :] < mine(leaf_ranks[:, 0])[:, None]).astype(
        jnp.float32
    )
    far_rows = swapped(side(rows, 1 - parity))
    far_coords = swapped(side(coords, 1 - parity))
    full = jnp.einsum("lvnk,lvnj->lkj", rows, rows, preferred_element_type=jnp.float32)
    eye = jnp.eye(rank_width, dtype=jnp.float32)
    gram = full * keep[:, :, None] * keep[:, None, :] + eye * (1.0 - keep)[:, None, :]
    upper, inverse = factor(gram, rank_width)
    upper = upper * keep[:, :, None]
    inverse = inverse * keep[:, :, None]
    every = lax.all_gather(inverse.reshape(sides, each, rank_width, rank_width), "gen", axis=1)
    every = every.reshape(leaf_count, rank_width, rank_width)

    factors = jnp.einsum(
        "lkj,ljp->lkp", upper, mine(translations[:, 0]).astype(jnp.float32), precision=HIGHEST
    )
    sums = covariance(
        jnp.concatenate([coords, side(coords, parity)], 0),
        jnp.concatenate([coords, far_coords], 0),
        jnp.concatenate([rows, side(rows, parity)], 0),
        jnp.concatenate([rows, far_rows], 0),
    )
    blocks = sandwich(inverse, sums[:owned] + NUGGET * full, inverse)
    bases = jnp.einsum(
        "lvnk,ljk->lvnj", local, every, precision=HIGHEST, preferred_element_type=jnp.float32
    )

    leaf_share = rank_width // gens
    leaf_pack = blocks.reshape(owned, gens, leaf_share, rank_width).transpose(1, 0, 2, 3)
    leaf_pack = lax.all_to_all(leaf_pack, "gen", split_axis=0, concat_axis=0, tiled=True)
    leaf_out = leaf_pack.reshape(gens, sides, each, leaf_share, rank_width)
    leaf_out = leaf_out.transpose(1, 0, 2, 3, 4).reshape(leaf_count, leaf_share, rank_width)

    given = jnp.concatenate([factors, blocks, inverse], 2)
    far = swapped(side(given, 1 - parity))
    own_factor, own_block = side(factors, parity), side(blocks, parity)
    far_factor = far[:, :, :parent_width]
    far_block = far[:, :, parent_width : parent_width + rank_width]
    far_inverse = far[:, :, parent_width + rank_width :]
    coupled = sandwich(side(inverse, parity), sums[owned:], far_inverse)
    coupled = jnp.where(is_even, coupled, jnp.swapaxes(coupled, 1, 2))
    even_block = jnp.where(is_even, own_block, far_block)
    odd_block = jnp.where(is_even, far_block, own_block)
    even_factor = jnp.where(is_even, own_factor, far_factor)
    odd_factor = jnp.where(is_even, far_factor, own_factor)
    ranks = parent_ranks[:, 0]
    if sides == 1:
        other = swapped(ranks)
        ranks = jnp.where(
            is_even, jnp.concatenate([ranks, other]), jnp.concatenate([other, ranks])
        )
    ranks = lax.dynamic_slice_in_dim(ranks, spot * each, each, 0)
    parent_keep = (lax.iota(jnp.int32, parent_width)[None, :] < ranks[:, None]).astype(jnp.float32)
    stacked = jnp.concatenate([even_factor, odd_factor], 1) * parent_keep[:, None, :]
    parent_gram = jnp.einsum("lak,laj->lkj", stacked, stacked, precision=HIGHEST)
    parent_gram = parent_gram + jnp.eye(parent_width, dtype=jnp.float32) * (1.0 - parent_keep)[:, None, :]
    _, parent_inverse = factor(parent_gram, parent_most)
    parent_bases = jnp.einsum("lak,ljk->laj", stacked, parent_inverse, precision=HIGHEST)
    top_row = jnp.concatenate([even_block, coupled], 2)
    bottom_row = jnp.concatenate([jnp.swapaxes(coupled, 1, 2), odd_block], 2)
    parent_matrix = jnp.concatenate([top_row, bottom_row], 1)
    mixed = jnp.einsum("lab,lbj->laj", parent_matrix, parent_bases, precision=HIGHEST)
    parent_blocks = jnp.einsum("lak,laj->lkj", parent_bases, mixed, precision=HIGHEST)

    basis_share = 2 * rank_width // gens
    parent_share = parent_width // gens
    tiles = parent_width // LANES

    def packed(values, share):
        values = values.reshape(each, gens, share, tiles, LANES)
        return values.transpose(1, 0, 3, 2, 4).reshape(gens, each * tiles * share, LANES)

    def unpacked(values, share):
        values = values.reshape(gens * each, tiles, share, LANES)
        if sides == 1:
            values = lax.dynamic_slice_in_dim(values, parity * half, half, 0)
        return values.transpose(0, 2, 1, 3).reshape(half, share, parent_width)

    pack = jnp.concatenate(
        [packed(parent_bases, basis_share), packed(parent_blocks, parent_share)], 1
    )
    pack = lax.all_to_all(pack, "gen", split_axis=0, concat_axis=0, tiled=True)
    second = each * tiles * basis_share
    basis_out = unpacked(pack[:, :second], basis_share)
    block_out = unpacked(pack[:, second:], parent_share)
    return (bases[:, None], leaf_out[:, None], basis_out[:, None], block_out[:, None])


def solution(mesh):
    return jax.shard_map(
        per_device,
        mesh=mesh,
        in_specs=(
            P(None, "leaf", None, None),
            P(None, "leaf", None, "gen", None),
            P(None, "leaf"),
            P(None, "leaf", None, None),
            P(None, "leaf"),
        ),
        out_specs=(
            P(None, "leaf", None, "gen", None),
            P(None, "leaf", "gen", None),
            P(None, "leaf", "gen", None),
            P(None, "leaf", "gen", None),
        ),
        check_vma=False,
    )
```

```python
import functools

import jax
import jax.numpy as jnp
from jax import lax
from jax.experimental import pallas as pl
from jax.experimental.pallas import tpu as pltpu
from jax.sharding import PartitionSpec as P

HIGHEST = lax.Precision.HIGHEST
RANGE_SCALE = 4.0
SIGMA_ONE = 1.0
SIGMA_TWO = 0.8
CROSS_CORR = 0.5
NUGGET = 0.1
BLOCK = 32
GROUP = 4
LANES = 128
TILE = 512
TINY = 1e-30


def swapped(array):
    return lax.ppermute(array, "leaf", [(i, i ^ 1) for i in range(lax.axis_size("leaf"))])


def eliminate(steps, gram_ref, upper_ref, inverse_ref, work_ref):
    count, rows, width = gram_ref.shape
    lanes = lax.broadcasted_iota(jnp.int32, (1, 1, width), 2)
    work_ref[...] = gram_ref[:, :steps, :]
    if steps < rows:
        upper_ref[:, steps:, :] = jnp.zeros((count, rows - steps, width), jnp.float32)
        inverse_ref[:, steps:, :] = jnp.zeros((count, rows - steps, width), jnp.float32)

    for start in range(0, steps, BLOCK):
        tile = start // LANES * LANES

        def step(turn, carry, start=start, tile=tile):
            first = start + turn * GROUP
            here = [lanes == first + i for i in range(GROUP)]
            spot = [mark[:, :, tile : tile + LANES] for mark in here]
            below = work_ref[:, start:, :]
            rows = [work_ref[:, pl.ds(first + i, 1), :] for i in range(GROUP)]

            def pick(values, i):
                values = values[:, :, tile : tile + LANES]
                return jnp.sum(jnp.where(spot[i], values, 0.0), axis=2, keepdims=True)

            columns = [pick(below, i) for i in range(GROUP)]
            corner = [[pick(rows[i], j) if j >= i else None for j in range(GROUP)] for i in range(GROUP)]
            for i in range(GROUP):
                pivot, row = corner[i][i], rows[i]
                root = lax.rsqrt(pivot)
                root = root * (1.5 - 0.5 * pivot * root * root)
                recip = root * root
                upper_ref[:, pl.ds(first + i, 1), :] = jnp.where(lanes >= first + i, row, 0.0) * root
                one = jnp.where(here[i], 1.0, 0.0)
                inverse_ref[:, pl.ds(first + i, 1), :] = jnp.where(lanes < first + i, row, one) * root
                scaled = columns[i] * recip
                below = jnp.where(here[i], -scaled, below - scaled * row)
                for j in range(i + 1, GROUP):
                    ratio = corner[i][j] * recip
                    rows[j] = jnp.where(here[i], -ratio, rows[j] - ratio * row)
                    columns[j] = columns[j] - scaled * corner[i][j]
                    for m in range(j, GROUP):
                        corner[j][m] = corner[j][m] - ratio * corner[i][m]
            work_ref[:, start:, :] = below
            return carry

        lax.fori_loop(0, BLOCK // GROUP, step, 0)


def factor(gram, steps):
    shape = jax.ShapeDtypeStruct(gram.shape, jnp.float32)
    count, _, width = gram.shape
    return pl.pallas_call(
        functools.partial(eliminate, steps),
        out_shape=(shape, shape),
        scratch_shapes=[pltpu.VMEM((count, steps, width), jnp.float32)],
    )(gram)


def split(value):
    high = value.astype(jnp.bfloat16)
    return high, (value - high.astype(jnp.float32)).astype(jnp.bfloat16)


def times(value, exact):
    high, low = split(value)
    return jnp.dot(high, exact, preferred_element_type=jnp.float32) + jnp.dot(
        low, exact, preferred_element_type=jnp.float32
    )


def gather_covariance(near_ref, far_ref, near_rows_ref, far_rows_ref, out_ref):
    @pl.when(pl.program_id(1) == 0)
    def _():
        out_ref[...] = jnp.zeros_like(out_ref)

    near = near_ref[0]
    far = far_ref[0]
    across = near[:, 0:1] - far[0:1, :]
    upward = near[:, 1:2] - far[1:2, :]
    square = across * across + upward * upward
    scaled = RANGE_SCALE * square * lax.rsqrt(jnp.maximum(square, TINY))
    decays = jnp.exp(-scaled)
    one = SIGMA_ONE * SIGMA_ONE * decays
    middle = (CROSS_CORR * SIGMA_ONE * SIGMA_TWO) * (1.0 + scaled) * decays
    smooth = (SIGMA_TWO * SIGMA_TWO) * (1.0 + scaled + scaled * scaled * (1.0 / 3.0)) * decays
    first, second = far_rows_ref[0, 0], far_rows_ref[0, 1]
    top = times(one, first) + times(middle, second)
    bottom = times(middle, first) + times(smooth, second)
    total = out_ref[0]
    for variable, image in ((0, top), (1, bottom)):
        for part in split(image):
            total = total + lax.dot_general(
                near_rows_ref[0, variable], part, (((0,), (0,)), ((), ())),
                preferred_element_type=jnp.float32,
            )
    out_ref[0] = total


def covariance(near_coords, far_coords, near_rows, far_rows):
    count, _, points, width = near_rows.shape
    tile = min(TILE, points)
    return pl.pallas_call(
        gather_covariance,
        grid=(count, points // tile),
        in_specs=[
            pl.BlockSpec((1, tile, 2), lambda i, j: (i, j, 0)),
            pl.BlockSpec((1, 2, points), lambda i, j: (i, 0, 0)),
            pl.BlockSpec((1, 2, tile, width), lambda i, j: (i, 0, j, 0)),
            pl.BlockSpec((1, 2, points, width), lambda i, j: (i, 0, 0, 0)),
        ],
        out_specs=pl.BlockSpec((1, width, width), lambda i, j: (i, 0, 0)),
        out_shape=jax.ShapeDtypeStruct((count, width, width), jnp.float32),
    )(jnp.swapaxes(near_coords, 1, 2), far_coords, near_rows, far_rows)


def sandwich(left, inner, right):
    mixed = jnp.einsum("lab,lcb->lac", inner, right, precision=HIGHEST)
    return jnp.einsum("lka,lac->lkc", left, mixed, precision=HIGHEST)


def per_device(points, generators, leaf_ranks, translations, parent_ranks):
    leaf_count, _, _, row_share, rank_width = generators.shape
    point_count = points.shape[-1]
    half = leaf_count // 2
    parent_width = translations.shape[-1]
    parent_most = parent_width * 5 // 8
    gens = lax.axis_size("gen")
    spot = lax.axis_index("gen")
    parity = lax.axis_index("leaf") % 2
    is_even = parity == 0
    sides = 2 if leaf_count // gens % 2 == 0 else 1
    each = leaf_count // (gens * sides)
    owned = sides * each

    def mine(values):
        values = values.reshape(sides, gens, each, *values.shape[1:])
        values = lax.dynamic_index_in_dim(values, spot, 1, keepdims=False)
        return values.reshape(owned, *values.shape[2:])

    def side(values, index):
        if sides == 1:
            return values
        return lax.dynamic_slice_in_dim(values, index * each, each, 0)

    local = generators[:, 0]
    spread = local.reshape(sides, gens, each, 2, row_share, rank_width)
    rows = lax.all_to_all(spread, "gen", split_axis=1, concat_axis=4, tiled=True)
    rows = rows.reshape(owned, 2, point_count, rank_width)
    coords = mine(points[:, 0])
    keep = (lax.iota(jnp.int32, rank_width)[None, :] < mine(leaf_ranks[:, 0])[:, None]).astype(
        jnp.float32
    )
    far_rows = swapped(side(rows, 1 - parity))
    far_coords = swapped(side(coords, 1 - parity))
    full = jnp.einsum("lvnk,lvnj->lkj", rows, rows, preferred_element_type=jnp.float32)
    eye = jnp.eye(rank_width, dtype=jnp.float32)
    gram = full * keep[:, :, None] * keep[:, None, :] + eye * (1.0 - keep)[:, None, :]
    upper, inverse = factor(gram, rank_width)
    upper = upper * keep[:, :, None]
    inverse = inverse * keep[:, :, None]
    every = lax.all_gather(inverse.reshape(sides, each, rank_width, rank_width), "gen", axis=1)
    every = every.reshape(leaf_count, rank_width, rank_width)

    factors = jnp.einsum(
        "lkj,ljp->lkp", upper, mine(translations[:, 0]).astype(jnp.float32), precision=HIGHEST
    )
    sums = covariance(coords, coords, rows, rows)
    crossed = covariance(side(coords, parity), far_coords, side(rows, parity), far_rows)
    blocks = sandwich(inverse, sums + NUGGET * full, inverse)
    bases = jnp.einsum(
        "lvnk,ljk->lvnj", local, every, precision=HIGHEST, preferred_element_type=jnp.float32
    )

    leaf_share = rank_width // gens
    leaf_pack = blocks.reshape(owned, gens, leaf_share, rank_width).transpose(1, 0, 2, 3)
    leaf_pack = lax.all_to_all(leaf_pack, "gen", split_axis=0, concat_axis=0, tiled=True)
    leaf_out = leaf_pack.reshape(gens, sides, each, leaf_share, rank_width)
    leaf_out = leaf_out.transpose(1, 0, 2, 3, 4).reshape(leaf_count, leaf_share, rank_width)

    given = jnp.concatenate([factors, blocks, inverse], 2)
    far = swapped(side(given, 1 - parity))
    own_factor, own_block = side(factors, parity), side(blocks, parity)
    far_factor = far[:, :, :parent_width]
    far_block = far[:, :, parent_width : parent_width + rank_width]
    far_inverse = far[:, :, parent_width + rank_width :]
    coupled = sandwich(side(inverse, parity), crossed, far_inverse)
    coupled = jnp.where(is_even, coupled, jnp.swapaxes(coupled, 1, 2))
    even_block = jnp.where(is_even, own_block, far_block)
    odd_block = jnp.where(is_even, far_block, own_block)
    even_factor = jnp.where(is_even, own_factor, far_factor)
    odd_factor = jnp.where(is_even, far_factor, own_factor)
    ranks = parent_ranks[:, 0]
    if sides == 1:
        other = swapped(ranks)
        ranks = jnp.where(
            is_even, jnp.concatenate([ranks, other]), jnp.concatenate([other, ranks])
        )
    ranks = lax.dynamic_slice_in_dim(ranks, spot * each, each, 0)
    parent_keep = (lax.iota(jnp.int32, parent_width)[None, :] < ranks[:, None]).astype(jnp.float32)
    stacked = jnp.concatenate([even_factor, odd_factor], 1) * parent_keep[:, None, :]
    parent_gram = jnp.einsum("lak,laj->lkj", stacked, stacked, precision=HIGHEST)
    parent_gram = parent_gram + jnp.eye(parent_width, dtype=jnp.float32) * (1.0 - parent_keep)[:, None, :]
    _, parent_inverse = factor(parent_gram, parent_most)
    parent_bases = jnp.einsum("lak,ljk->laj", stacked, parent_inverse, precision=HIGHEST)
    top_row = jnp.concatenate([even_block, coupled], 2)
    bottom_row = jnp.concatenate([jnp.swapaxes(coupled, 1, 2), odd_block], 2)
    parent_matrix = jnp.concatenate([top_row, bottom_row], 1)
    mixed = jnp.einsum("lab,lbj->laj", parent_matrix, parent_bases, precision=HIGHEST)
    parent_blocks = jnp.einsum("lak,laj->lkj", parent_bases, mixed, precision=HIGHEST)

    basis_share = 2 * rank_width // gens
    parent_share = parent_width // gens

    def packed(values, share):
        values = values.reshape(each, gens, share, parent_width)
        return values.transpose(1, 0, 2, 3).reshape(gens, each * share, parent_width)

    def unpacked(values, share):
        values = values.reshape(gens * each, share, parent_width)
        if sides == 1:
            values = lax.dynamic_slice_in_dim(values, parity * half, half, 0)
        return values

    pack = jnp.concatenate(
        [packed(parent_bases, basis_share), packed(parent_blocks, parent_share)], 1
    )
    pack = lax.all_to_all(pack, "gen", split_axis=0, concat_axis=0, tiled=True)
    second = each * basis_share
    basis_out = unpacked(pack[:, :second], basis_share)
    block_out = unpacked(pack[:, second:], parent_share)
    return (bases[:, None], leaf_out[:, None], basis_out[:, None], block_out[:, None])


def solution(mesh):
    return jax.shard_map(
        per_device,
        mesh=mesh,
        in_specs=(
            P(None, "leaf", None, None),
            P(None, "leaf", None, "gen", None),
            P(None, "leaf"),
            P(None, "leaf", None, None),
            P(None, "leaf"),
        ),
        out_specs=(
            P(None, "leaf", None, "gen", None),
            P(None, "leaf", "gen", None),
            P(None, "leaf", "gen", None),
            P(None, "leaf", "gen", None),
        ),
        check_vma=False,
    )
```

```python
import functools

import jax
import jax.numpy as jnp
from jax import lax
from jax.experimental import pallas as pl
from jax.experimental.pallas import tpu as pltpu
from jax.sharding import PartitionSpec as P

HIGHEST = lax.Precision.HIGHEST
RANGE_SCALE = 4.0
SIGMA_ONE = 1.0
SIGMA_TWO = 0.8
CROSS_CORR = 0.5
NUGGET = 0.1
BLOCK = 16
GROUP = 4
LANES = 128
TILE = 512
TINY = 1e-30


def swapped(array):
    return lax.ppermute(array, "leaf", [(i, i ^ 1) for i in range(lax.axis_size("leaf"))])


def eliminate(steps, gram_ref, upper_ref, inverse_ref, work_ref):
    count, rows, width = gram_ref.shape
    lanes = lax.broadcasted_iota(jnp.int32, (1, 1, width), 2)
    work_ref[...] = gram_ref[:, :steps, :]
    if steps < rows:
        upper_ref[:, steps:, :] = jnp.zeros((count, rows - steps, width), jnp.float32)
        inverse_ref[:, steps:, :] = jnp.zeros((count, rows - steps, width), jnp.float32)

    for start in range(0, steps, BLOCK):
        tile = start // LANES * LANES

        def step(turn, carry, start=start, tile=tile):
            first = start + turn * GROUP
            here = [lanes == first + i for i in range(GROUP)]
            spot = [mark[:, :, tile : tile + LANES] for mark in here]
            below = work_ref[:, start:, :]
            rows = [work_ref[:, pl.ds(first + i, 1), :] for i in range(GROUP)]

            def pick(values, i):
                values = values[:, :, tile : tile + LANES]
                return jnp.sum(jnp.where(spot[i], values, 0.0), axis=2, keepdims=True)

            columns = [pick(below, i) for i in range(GROUP)]
            corner = [[pick(rows[i], j) if j >= i else None for j in range(GROUP)] for i in range(GROUP)]
            for i in range(GROUP):
                pivot, row = corner[i][i], rows[i]
                root = lax.rsqrt(pivot)
                root = root * (1.5 - 0.5 * pivot * root * root)
                recip = root * root
                upper_ref[:, pl.ds(first + i, 1), :] = jnp.where(lanes >= first + i, row, 0.0) * root
                one = jnp.where(here[i], 1.0, 0.0)
                inverse_ref[:, pl.ds(first + i, 1), :] = jnp.where(lanes < first + i, row, one) * root
                scaled = columns[i] * recip
                below = jnp.where(here[i], -scaled, below - scaled * row)
                for j in range(i + 1, GROUP):
                    ratio = corner[i][j] * recip
                    rows[j] = jnp.where(here[i], -ratio, rows[j] - ratio * row)
                    columns[j] = columns[j] - scaled * corner[i][j]
                    for m in range(j, GROUP):
                        corner[j][m] = corner[j][m] - ratio * corner[i][m]
            work_ref[:, start:, :] = below
            return carry

        lax.fori_loop(0, BLOCK // GROUP, step, 0)


def factor(gram, steps):
    shape = jax.ShapeDtypeStruct(gram.shape, jnp.float32)
    count, _, width = gram.shape
    return pl.pallas_call(
        functools.partial(eliminate, steps),
        out_shape=(shape, shape),
        scratch_shapes=[pltpu.VMEM((count, steps, width), jnp.float32)],
    )(gram)


def split(value):
    high = value.astype(jnp.bfloat16)
    return high, (value - high.astype(jnp.float32)).astype(jnp.bfloat16)


def times(value, exact):
    high, low = split(value)
    return jnp.dot(high, exact, preferred_element_type=jnp.float32) + jnp.dot(
        low, exact, preferred_element_type=jnp.float32
    )


def gather_covariance(near_ref, far_ref, near_rows_ref, far_rows_ref, out_ref):
    @pl.when(pl.program_id(1) == 0)
    def _():
        out_ref[...] = jnp.zeros_like(out_ref)

    near = near_ref[0]
    far = far_ref[0]
    across = near[:, 0:1] - far[0:1, :]
    upward = near[:, 1:2] - far[1:2, :]
    square = across * across + upward * upward
    scaled = RANGE_SCALE * square * lax.rsqrt(jnp.maximum(square, TINY))
    decays = jnp.exp(-scaled)
    one = SIGMA_ONE * SIGMA_ONE * decays
    middle = (CROSS_CORR * SIGMA_ONE * SIGMA_TWO) * (1.0 + scaled) * decays
    smooth = (SIGMA_TWO * SIGMA_TWO) * (1.0 + scaled + scaled * scaled * (1.0 / 3.0)) * decays
    first, second = far_rows_ref[0, 0], far_rows_ref[0, 1]
    top = times(one, first) + times(middle, second)
    bottom = times(middle, first) + times(smooth, second)
    total = out_ref[0]
    for variable, image in ((0, top), (1, bottom)):
        for part in split(image):
            total = total + lax.dot_general(
                near_rows_ref[0, variable], part, (((0,), (0,)), ((), ())),
                preferred_element_type=jnp.float32,
            )
    out_ref[0] = total


def covariance(near_coords, far_coords, near_rows, far_rows):
    count, _, points, width = near_rows.shape
    tile = min(TILE, points)
    return pl.pallas_call(
        gather_covariance,
        grid=(count, points // tile),
        in_specs=[
            pl.BlockSpec((1, tile, 2), lambda i, j: (i, j, 0)),
            pl.BlockSpec((1, 2, points), lambda i, j: (i, 0, 0)),
            pl.BlockSpec((1, 2, tile, width), lambda i, j: (i, 0, j, 0)),
            pl.BlockSpec((1, 2, points, width), lambda i, j: (i, 0, 0, 0)),
        ],
        out_specs=pl.BlockSpec((1, width, width), lambda i, j: (i, 0, 0)),
        out_shape=jax.ShapeDtypeStruct((count, width, width), jnp.float32),
    )(jnp.swapaxes(near_coords, 1, 2), far_coords, near_rows, far_rows)


def sandwich(left, inner, right):
    mixed = jnp.einsum("lab,lcb->lac", inner, right, precision=HIGHEST)
    return jnp.einsum("lka,lac->lkc", left, mixed, precision=HIGHEST)


def per_device(points, generators, leaf_ranks, translations, parent_ranks):
    leaf_count, _, _, row_share, rank_width = generators.shape
    point_count = points.shape[-1]
    half = leaf_count // 2
    parent_width = translations.shape[-1]
    parent_most = parent_width * 5 // 8
    gens = lax.axis_size("gen")
    spot = lax.axis_index("gen")
    parity = lax.axis_index("leaf") % 2
    is_even = parity == 0
    sides = 2 if leaf_count // gens % 2 == 0 else 1
    each = leaf_count // (gens * sides)
    owned = sides * each

    def mine(values):
        values = values.reshape(sides, gens, each, *values.shape[1:])
        values = lax.dynamic_index_in_dim(values, spot, 1, keepdims=False)
        return values.reshape(owned, *values.shape[2:])

    def side(values, index):
        if sides == 1:
            return values
        return lax.dynamic_slice_in_dim(values, index * each, each, 0)

    local = generators[:, 0]
    spread = local.reshape(sides, gens, each, 2, row_share, rank_width)
    rows = lax.all_to_all(spread, "gen", split_axis=1, concat_axis=4, tiled=True)
    rows = rows.reshape(owned, 2, point_count, rank_width)
    coords = mine(points[:, 0])
    keep = (lax.iota(jnp.int32, rank_width)[None, :] < mine(leaf_ranks[:, 0])[:, None]).astype(
        jnp.float32
    )
    far_rows = swapped(side(rows, 1 - parity))
    far_coords = swapped(side(coords, 1 - parity))
    full = jnp.einsum("lvnk,lvnj->lkj", rows, rows, preferred_element_type=jnp.float32)
    eye = jnp.eye(rank_width, dtype=jnp.float32)
    gram = full * keep[:, :, None] * keep[:, None, :] + eye * (1.0 - keep)[:, None, :]
    upper, inverse = factor(gram, rank_width)
    upper = upper * keep[:, :, None]
    inverse = inverse * keep[:, :, None]
    every = lax.all_gather(inverse.reshape(sides, each, rank_width, rank_width), "gen", axis=1)
    every = every.reshape(leaf_count, rank_width, rank_width)

    factors = jnp.einsum(
        "lkj,ljp->lkp", upper, mine(translations[:, 0]).astype(jnp.float32), precision=HIGHEST
    )
    sums = covariance(coords, coords, rows, rows)
    crossed = covariance(side(coords, parity), far_coords, side(rows, parity), far_rows)
    blocks = sandwich(inverse, sums + NUGGET * full, inverse)
    bases = jnp.einsum(
        "lvnk,ljk->lvnj", local, every, precision=HIGHEST, preferred_element_type=jnp.float32
    )

    leaf_share = rank_width // gens
    leaf_pack = blocks.reshape(owned, gens, leaf_share, rank_width).transpose(1, 0, 2, 3)
    leaf_pack = lax.all_to_all(leaf_pack, "gen", split_axis=0, concat_axis=0, tiled=True)
    leaf_out = leaf_pack.reshape(gens, sides, each, leaf_share, rank_width)
    leaf_out = leaf_out.transpose(1, 0, 2, 3, 4).reshape(leaf_count, leaf_share, rank_width)

    given = jnp.concatenate([factors, blocks, inverse], 2)
    far = swapped(side(given, 1 - parity))
    own_factor, own_block = side(factors, parity), side(blocks, parity)
    far_factor = far[:, :, :parent_width]
    far_block = far[:, :, parent_width : parent_width + rank_width]
    far_inverse = far[:, :, parent_width + rank_width :]
    coupled = sandwich(side(inverse, parity), crossed, far_inverse)
    coupled = jnp.where(is_even, coupled, jnp.swapaxes(coupled, 1, 2))
    even_block = jnp.where(is_even, own_block, far_block)
    odd_block = jnp.where(is_even, far_block, own_block)
    even_factor = jnp.where(is_even, own_factor, far_factor)
    odd_factor = jnp.where(is_even, far_factor, own_factor)
    ranks = parent_ranks[:, 0]
    if sides == 1:
        other = swapped(ranks)
        ranks = jnp.where(
            is_even, jnp.concatenate([ranks, other]), jnp.concatenate([other, ranks])
        )
    ranks = lax.dynamic_slice_in_dim(ranks, spot * each, each, 0)
    parent_keep = (lax.iota(jnp.int32, parent_width)[None, :] < ranks[:, None]).astype(jnp.float32)
    stacked = jnp.concatenate([even_factor, odd_factor], 1) * parent_keep[:, None, :]
    parent_gram = jnp.einsum("lak,laj->lkj", stacked, stacked, precision=HIGHEST)
    parent_gram = parent_gram + jnp.eye(parent_width, dtype=jnp.float32) * (1.0 - parent_keep)[:, None, :]
    _, parent_inverse = factor(parent_gram, parent_most)
    parent_bases = jnp.einsum("lak,ljk->laj", stacked, parent_inverse, precision=HIGHEST)
    top_row = jnp.concatenate([even_block, coupled], 2)
    bottom_row = jnp.concatenate([jnp.swapaxes(coupled, 1, 2), odd_block], 2)
    parent_matrix = jnp.concatenate([top_row, bottom_row], 1)
    mixed = jnp.einsum("lab,lbj->laj", parent_matrix, parent_bases, precision=HIGHEST)
    parent_blocks = jnp.einsum("lak,laj->lkj", parent_bases, mixed, precision=HIGHEST)

    basis_share = 2 * rank_width // gens
    parent_share = parent_width // gens

    def packed(values, share):
        values = values.reshape(each, gens, share, parent_width)
        return values.transpose(1, 0, 2, 3).reshape(gens, each * share, parent_width)

    def unpacked(values, share):
        values = values.reshape(gens * each, share, parent_width)
        if sides == 1:
            values = lax.dynamic_slice_in_dim(values, parity * half, half, 0)
        return values

    pack = jnp.concatenate(
        [packed(parent_bases, basis_share), packed(parent_blocks, parent_share)], 1
    )
    pack = lax.all_to_all(pack, "gen", split_axis=0, concat_axis=0, tiled=True)
    second = each * basis_share
    basis_out = unpacked(pack[:, :second], basis_share)
    block_out = unpacked(pack[:, second:], parent_share)
    return (bases[:, None], leaf_out[:, None], basis_out[:, None], block_out[:, None])


def solution(mesh):
    return jax.shard_map(
        per_device,
        mesh=mesh,
        in_specs=(
            P(None, "leaf", None, None),
            P(None, "leaf", None, "gen", None),
            P(None, "leaf"),
            P(None, "leaf", None, None),
            P(None, "leaf"),
        ),
        out_specs=(
            P(None, "leaf", None, "gen", None),
            P(None, "leaf", "gen", None),
            P(None, "leaf", "gen", None),
            P(None, "leaf", "gen", None),
        ),
        check_vma=False,
    )
```
